32 devices in a mesh: frame: 4 (over y, x), seq: 8 (over z, core).
Axes of the slice: x: 2, y: 2, z: 4, core: 2. Of those that a mesh axis runs over, the one named last changes fastest.
Arguments:
- vid_q: bfloat16 [4, 256, 2048], P('frame', 'seq'), may hold values from -6 to 6
- vid_k: bfloat16 [4, 256, 2048], P('frame', 'seq'), may hold values from -6 to 6
- vid_v: bfloat16 [4, 256, 2048], P('frame', 'seq'), may hold values from -6 to 6
- vid_dout: bfloat16 [4, 256, 2048], P('frame', 'seq'), may hold values from -6 to 6
- aud_q: bfloat16 [4, 768, 2048], P('frame', 'seq'), may hold values from -6 to 6
- aud_k: bfloat16 [4, 768, 2048], P('frame', 'seq'), may hold values from -6 to 6
- aud_v: bfloat16 [4, 768, 2048], P('frame', 'seq'), may hold values from -6 to 6
- aud_dout: bfloat16 [4, 768, 2048], P('frame', 'seq'), may hold values from -6 to 6
- aud_len: int32 [4, 8], replicated, may hold values from 32 to 96, as said below
- match: int32 [4], replicated, may hold values from 0 to 3, each once
Outputs:
- d_vid_q: bfloat16 [4, 256, 2048], P('frame', 'seq')
- d_vid_k: bfloat16 [4, 256, 2048], P('frame', 'seq')
- d_vid_v: bfloat16 [4, 256, 2048], P('frame', 'seq')
- d_aud_q: bfloat16 [4, 768, 2048], P('frame', 'seq')
- d_aud_k: bfloat16 [4, 768, 2048], P('frame', 'seq')
- d_aud_v: bfloat16 [4, 768, 2048], P('frame', 'seq')
The draws below stay inside these ranges and needn't reach their ends.
Inputs may be any that keep to these rules, and one draw needn't show every extreme that they name: `aud_len`: every entry is a whole multiple of 32; in every frame group one time block has 96 live slots and another has 32. match names every frame group once.
All inputs are finite; a program needn't handle non-finite values.
Results may differ from the reference program's by a relative error of at most 0.012.
The reference program's roundings to bfloat16 on the way count: a program that leaves them out, or rounds other values in their place, can miss the bound.
Values may be sent and summed in bfloat16 or wider, within the bound.
A program may use at most 64 MiB of HBM per device.

```python
import jax
import jax.numpy as jnp
from jax import lax

HEADS = 16
HD = 128
VDEV = 32
ATILE = 32
LTILES = 3
BAND = 2
ACAP = 96
FRAMES = 4
SEQS = 8
VTOK = 256
ATOK = 768


def draw_aud_len(key, part):
    tiles = jax.random.randint(jax.random.fold_in(key, 11), (FRAMES, SEQS), 1, LTILES + 1)
    first = jax.random.randint(jax.random.fold_in(key, 12), (FRAMES,), 0, SEQS)
    stride = jax.random.randint(jax.random.fold_in(key, 13), (FRAMES,), 1, SEQS)
    second = (first + stride) % SEQS
    columns = jnp.arange(SEQS)[None, :]
    tiles = jnp.where(columns == first[:, None], LTILES, tiles)
    tiles = jnp.where(columns == second[:, None], 1, tiles)
    return (tiles * ATILE).astype(jnp.int32)


def drawn_rows(key, own, rows):
    values = jax.random.normal(jax.random.fold_in(key, own), (FRAMES, SEQS * rows, HEADS * HD), jnp.float32)
    return jnp.clip(values, -6.0, 6.0)


def draw_vid_q(key, part):
    values = drawn_rows(key, 21, VDEV)
    return values.astype(jnp.bfloat16)


def draw_aud_k(key, part):
    values = drawn_rows(key, 22, ACAP)
    return values.astype(jnp.bfloat16)


def draw_aud_q(key, part):
    values = drawn_rows(key, 23, ACAP)
    return values.astype(jnp.bfloat16)


def draw_vid_k(key, part):
    values = drawn_rows(key, 24, VDEV)
    return values.astype(jnp.bfloat16)


def level_of(stream_key, shape, split, low, high):
    def one(dim, shards_of):
        steps = jax.random.uniform(jax.random.fold_in(jax.random.fold_in(stream_key, 6), dim), (shards_of,), jnp.float32, low / len(split), high / len(split))
        return jnp.repeat(jnp.exp(steps), shape[dim] // shards_of).reshape((-1,) + (1,) * (len(shape) - dim - 1))

    level = one(*split[0])
    for cut in split[1:]:
        level = level * one(*cut)
    return level


def scatter_about(rng, extent, spread, bound, shards=(), kind=jnp.bfloat16):
    values = jax.random.normal(rng, extent, jnp.float32) * spread
    if len(shards) > 0:
        values = level_of(rng, extent, shards, -0.22, 0.18) * values
    return jnp.clip(values, min=-bound, max=bound).astype(kind)


def setup_inputs(seed: int = 0) -> dict:
    key_list = jax.random.split(jax.random.key(seed), 11)
    return {
        "vid_q": draw_vid_q(jax.random.fold_in(key_list[10], 71), 0),
        "vid_k": draw_vid_k(jax.random.fold_in(key_list[10], 71), 0),
        "vid_v": scatter_about(key_list[2], (FRAMES, VTOK, HEADS * HD), 1.0, 6.0, ((0, 4), (1, 8))),
        "vid_dout": scatter_about(key_list[3], (FRAMES, VTOK, HEADS * HD), 1.0, 6.0, ((0, 4), (1, 8))),
        "aud_q": draw_aud_q(jax.random.fold_in(key_list[10], 71), 0),
        "aud_k": draw_aud_k(jax.random.fold_in(key_list[10], 71), 0),
        "aud_v": scatter_about(key_list[6], (FRAMES, ATOK, HEADS * HD), 1.0, 6.0, ((0, 4), (1, 8))),
        "aud_dout": scatter_about(key_list[7], (FRAMES, ATOK, HEADS * HD), 1.0, 6.0, ((0, 4), (1, 8))),
        "aud_len": draw_aud_len(jax.random.fold_in(key_list[10], 71), 0),
        "match": jax.random.permutation(key_list[9], FRAMES).astype(jnp.int32),
    }


NEG_BIG = -1e30


def window(blocks):
    padded = jnp.pad(blocks, [(BAND, BAND)] + [(0, 0)] * (blocks.ndim - 1))
    count = blocks.shape[0]
    return jnp.concatenate([padded[position:position + count] for position in range(2 * BAND + 1)], axis=1)


def attend_pair(queries, key_rows, val_rows, grad_out, key_mask):
    factor = HD ** -0.5
    single = jnp.float32
    query_wide = queries.astype(single)
    key_wide = key_rows.astype(single)
    value_wide = val_rows.astype(single)
    grad_wide = grad_out.astype(single)
    scores = jnp.einsum('bqhd,bkhd->bhqk', query_wide, key_wide) * factor
    scores = jnp.where(key_mask[:, None, None, :], scores, NEG_BIG)
    largest = jnp.max(scores, axis=-1, keepdims=True)
    exponent = jnp.exp(scores - largest)
    weights = exponent / jnp.sum(exponent, axis=-1, keepdims=True)
    weights_half = weights.astype(jnp.bfloat16)
    weights_back = weights_half.astype(single)
    output = jnp.einsum('bhqk,bkhd->bqhd', weights_back, value_wide)
    deltas = jnp.transpose(jnp.sum(grad_wide * output, axis=-1), (0, 2, 1))[..., None]
    grad_weights = jnp.einsum('bqhd,bkhd->bhqk', grad_wide, value_wide)
    grad_scores = (weights * (grad_weights - deltas)).astype(jnp.bfloat16)
    scores_back = grad_scores.astype(single)
    grad_query = jnp.einsum('bhqk,bkhd->bqhd', scores_back, key_wide) * factor
    grad_key = jnp.einsum('bhqk,bqhd->bkhd', scores_back, query_wide) * factor
    grad_value = jnp.einsum('bhqk,bqhd->bkhd', weights_back, grad_wide)
    return grad_query, grad_key, grad_value


def owner_sum(part, rows):
    count = part.shape[0]
    span = 2 * BAND + 1
    pieces = part.reshape((count, span, rows) + part.shape[2:])
    rounded = lax.optimization_barrier(pieces.astype(jnp.bfloat16)).astype(jnp.float32)
    result = jnp.zeros((count, rows) + part.shape[2:], jnp.float32)
    for position in range(span):
        padded = jnp.pad(rounded[:, position], [(BAND, BAND)] + [(0, 0)] * (part.ndim - 1))
        result = result + padded[2 * BAND - position:2 * BAND - position + count]
    return result


def reference(vid_q, vid_k, vid_v, vid_dout, aud_q, aud_k, aud_v, aud_dout, aud_len, match):
    order = jnp.arange(FRAMES, dtype=jnp.int32)
    inverse = jnp.sum(jnp.where(match[None, :] == order[:, None], order[None, :], 0), axis=1).astype(jnp.int32)
    lengths = jnp.take(aud_len, match, axis=0)
    slots = jnp.arange(ACAP, dtype=jnp.int32)
    audio_mask = slots[None, None, :] < lengths[:, :, None]

    def blocks(array, rows):
        return array.reshape(FRAMES, SEQS, rows, HEADS, HD)

    def paired(array):
        return blocks(jnp.take(array, match, axis=0), ACAP)

    audio_grad = jnp.where(audio_mask[..., None, None], paired(aud_dout), jnp.zeros((), jnp.bfloat16))
    video_mask = window(jnp.ones((SEQS, VDEV), jnp.float32)) > 0.5

    def one_frame(items):
        video_query, video_key, video_value, video_grad, audio_query, audio_key, audio_value, audio_cot, audio_live = items
        audio_window = window(audio_live.astype(jnp.float32)) > 0.5
        grad_vq, grad_ak, grad_av = attend_pair(video_query, window(audio_key), window(audio_value), video_grad, audio_window)
        grad_aq, grad_vk, grad_vv = attend_pair(audio_query, window(video_key), window(video_value), audio_cot, video_mask)
        return (grad_vq, owner_sum(grad_vk, VDEV), owner_sum(grad_vv, VDEV),
                grad_aq, owner_sum(grad_ak, ACAP), owner_sum(grad_av, ACAP))

    results = lax.map(one_frame, (blocks(vid_q, VDEV), blocks(vid_k, VDEV), blocks(vid_v, VDEV), blocks(vid_dout, VDEV),
                                  paired(aud_q), paired(aud_k), paired(aud_v), audio_grad, audio_mask))

    def finish(array, rows):
        return array.reshape(FRAMES, SEQS * rows, HEADS * HD).astype(jnp.bfloat16)

    def unpair(array):
        return jnp.take(finish(array, ACAP), inverse, axis=0)

    return (finish(results[0], VDEV), finish(results[1], VDEV), finish(results[2], VDEV),
            unpair(results[3]), unpair(results[4]), unpair(results[5]))
```

```python
import jax
import jax.numpy as jnp
from jax import lax
from jax.sharding import PartitionSpec as P

HD = 128
BAND = 2


NEG_BIG = -1e30


def from_behind(x, axis, by):
    peers = lax.axis_size(axis)
    pairs = [(i, i + by) for i in range(peers) if 0 <= i + by < peers]
    return lax.ppermute(x, axis, pairs)


def picked(x, places):
    rows = [
        lax.dynamic_slice_in_dim(x, places[member], 1, 0) for member in range(places.shape[0])
    ]
    return jnp.concatenate(rows, axis=0)


def query_side(queries, key_rows, val_rows, grad_out, key_mask):
    factor = HD ** (-0.5)
    scores = (
        jnp.einsum("fhqd,fhkd->fhqk", queries, key_rows, preferred_element_type=jnp.float32)
        * factor
    )
    scores = jnp.where(key_mask[:, None, None, :], scores, NEG_BIG)
    largest = jnp.max(scores, axis=-1, keepdims=True)
    exponent = jnp.exp(scores - largest)
    totals = jnp.sum(exponent, axis=-1, keepdims=True)
    weights = exponent / totals
    weights_half = weights.astype(jnp.bfloat16)
    output = jnp.einsum(
        "fhqk,fhkd->fhqd", weights_half, val_rows, preferred_element_type=jnp.float32
    )
    deltas = jnp.sum(grad_out.astype(jnp.float32) * output, axis=-1, keepdims=True)
    grad_weights = jnp.einsum(
        "fhqd,fhkd->fhqk", grad_out, val_rows, preferred_element_type=jnp.float32
    )
    grad_scores = (weights * (grad_weights - deltas)).astype(jnp.bfloat16)
    grad_query = (
        jnp.einsum("fhqk,fhkd->fhqd", grad_scores, key_rows, preferred_element_type=jnp.float32)
        * factor
    )
    return (grad_query, weights_half, grad_scores, largest[..., 0], totals[..., 0], deltas[..., 0])


def shards(vid_q, vid_k, vid_v, vid_dout, aud_q, aud_k, aud_v, aud_dout, aud_len, match):
    frames = lax.axis_size("frame")
    seq_count = lax.axis_size("seq")
    here = lax.axis_index("seq")
    moved = (
        lax.all_to_all(vid_q, "frame", split_axis=2, concat_axis=0, tiled=True),
        lax.all_to_all(vid_k, "frame", split_axis=2, concat_axis=0, tiled=True),
        lax.all_to_all(vid_v, "frame", split_axis=2, concat_axis=0, tiled=True),
        lax.all_to_all(vid_dout, "frame", split_axis=2, concat_axis=0, tiled=True),
        lax.all_to_all(aud_q, "frame", split_axis=2, concat_axis=0, tiled=True),
        lax.all_to_all(aud_k, "frame", split_axis=2, concat_axis=0, tiled=True),
        lax.all_to_all(aud_v, "frame", split_axis=2, concat_axis=0, tiled=True),
        lax.all_to_all(aud_dout, "frame", split_axis=2, concat_axis=0, tiled=True),
    )
    order = jnp.arange(frames, dtype=jnp.int32)
    inverse = jnp.sum(jnp.where(match[None, :] == order[:, None], order[None, :], 0), axis=1)
    video_query, video_key, video_value, video_grad = (moved[0], moved[1], moved[2], moved[3])
    audio_query = picked(moved[4], match)
    audio_key = picked(moved[5], match)
    audio_value = picked(moved[6], match)
    audio_grad = picked(moved[7], match)
    lengths = picked(aud_len, match)
    video_rows = video_query.shape[1]
    audio_rows = audio_query.shape[1]
    width_here = video_query.shape[2]
    heads_here = width_here // HD
    slots = lax.broadcasted_iota(jnp.int32, (frames, audio_rows), 1)

    def inside(offset):
        target = here + offset
        return (target >= 0) & (target < seq_count)

    def audio_mask(offset):
        column = lax.dynamic_index_in_dim(
            lengths, jnp.clip(here + offset, 0, seq_count - 1), 1, keepdims=True
        )
        return (slots < column) & inside(offset)

    def video_mask(offset):
        return jnp.broadcast_to(inside(offset), (frames, video_rows))

    def split(array):
        shaped = array.reshape(array.shape[:-1] + (heads_here, HD))
        return jnp.moveaxis(shaped, -2, -3)

    def joined(array):
        moved_back = jnp.moveaxis(array, -3, -2)
        return moved_back.reshape(moved_back.shape[:-2] + (width_here,))

    offsets = list(range(-BAND, BAND + 1))
    audio_grad = jnp.where(audio_mask(0)[:, :, None], audio_grad, jnp.zeros((), jnp.bfloat16))
    audio_keys_mask = jnp.concatenate([audio_mask(offset) for offset in offsets], axis=1)
    video_keys_mask = jnp.concatenate([video_mask(offset) for offset in offsets], axis=1)
    factor = HD ** (-0.5)
    packed = jnp.concatenate(
        [jnp.stack([video_key, video_value]), jnp.stack([audio_key, audio_value])], axis=2
    )
    nearby = []
    for offset in offsets:
        if offset == 0:
            nearby.append(packed)
        else:
            nearby.append(from_behind(packed, "seq", -offset))
    video_window = jnp.concatenate([member[:, :, :video_rows] for member in nearby], axis=2)
    audio_window = jnp.concatenate([member[:, :, video_rows:] for member in nearby], axis=2)
    video_side = query_side(
        split(video_query),
        split(audio_window[0]),
        split(audio_window[1]),
        split(video_grad),
        audio_keys_mask,
    )
    audio_side = query_side(
        split(audio_query),
        split(video_window[0]),
        split(video_window[1]),
        split(audio_grad),
        video_keys_mask,
    )
    grad_vq = joined(video_side[0])
    grad_aq = joined(audio_side[0])
    audio_key_terms = (
        jnp.einsum(
            "fhqk,fhqd->fhkd", video_side[2], split(video_query), preferred_element_type=jnp.float32
        )
        * factor
    )
    audio_value_terms = jnp.einsum(
        "fhqk,fhqd->fhkd", video_side[1], split(video_grad), preferred_element_type=jnp.float32
    )
    video_key_terms = (
        jnp.einsum(
            "fhqk,fhqd->fhkd", audio_side[2], split(audio_query), preferred_element_type=jnp.float32
        )
        * factor
    )
    video_value_terms = jnp.einsum(
        "fhqk,fhqd->fhkd", audio_side[1], split(audio_grad), preferred_element_type=jnp.float32
    )
    video_terms = jnp.stack(
        [
            joined(video_key_terms).astype(jnp.bfloat16),
            joined(video_value_terms).astype(jnp.bfloat16),
        ]
    )
    audio_terms = jnp.stack(
        [
            joined(audio_key_terms).astype(jnp.bfloat16),
            joined(audio_value_terms).astype(jnp.bfloat16),
        ]
    )
    summed = jnp.zeros((2, frames, video_rows + audio_rows, width_here), jnp.float32)
    for position, offset in enumerate(offsets):
        piece = jnp.concatenate(
            [
                video_terms[:, :, position * video_rows : (position + 1) * video_rows],
                audio_terms[:, :, position * audio_rows : (position + 1) * audio_rows],
            ],
            axis=2,
        )
        if offset == 0:
            summed = summed + piece.astype(jnp.float32)
        else:
            summed = summed + from_behind(piece, "seq", offset).astype(jnp.float32)
    grad_vk = summed[0, :, :video_rows]
    grad_vv = summed[1, :, :video_rows]
    grad_ak = summed[0, :, video_rows:]
    grad_av = summed[1, :, video_rows:]
    grad_aq = picked(grad_aq, inverse)
    grad_ak = picked(grad_ak, inverse)
    grad_av = picked(grad_av, inverse)
    returned = (
        lax.all_to_all(
            grad_vq.astype(jnp.bfloat16), "frame", split_axis=0, concat_axis=2, tiled=True
        ),
        lax.all_to_all(
            grad_vk.astype(jnp.bfloat16), "frame", split_axis=0, concat_axis=2, tiled=True
        ),
        lax.all_to_all(
            grad_vv.astype(jnp.bfloat16), "frame", split_axis=0, concat_axis=2, tiled=True
        ),
        lax.all_to_all(
            grad_aq.astype(jnp.bfloat16), "frame", split_axis=0, concat_axis=2, tiled=True
        ),
        lax.all_to_all(
            grad_ak.astype(jnp.bfloat16), "frame", split_axis=0, concat_axis=2, tiled=True
        ),
        lax.all_to_all(
            grad_av.astype(jnp.bfloat16), "frame", split_axis=0, concat_axis=2, tiled=True
        ),
    )
    return (returned[0], returned[1], returned[2], returned[3], returned[4], returned[5])


def solution(mesh):
    return jax.shard_map(
        shards,
        mesh=mesh,
        in_specs=(
            P("frame", "seq", None),
            P("frame", "seq", None),
            P("frame", "seq", None),
            P("frame", "seq", None),
            P("frame", "seq", None),
            P("frame", "seq", None),
            P("frame", "seq", None),
            P("frame", "seq", None),
            P(),
            P(),
        ),
        out_specs=(
            P("frame", "seq", None),
            P("frame", "seq", None),
            P("frame", "seq", None),
            P("frame", "seq", None),
            P("frame", "seq", None),
            P("frame", "seq", None),
        ),
        check_vma=False,
    )
```

```python
import functools

import jax
import jax.numpy as jnp
from jax import lax
from jax.experimental import pallas as pl
from jax.experimental.pallas import tpu as pltpu
from jax.sharding import PartitionSpec as P

HD = 128
BAND = 2
SPAN = 2 * BAND + 1
NEG_BIG = -1e30


def from_behind(x, axis, by):
    peers = lax.axis_size(axis)
    pairs = [(i, i + by) for i in range(peers) if 0 <= i + by < peers]
    return lax.ppermute(x, axis, pairs)


def dot_nt(a, b):
    return lax.dot_general(a, b, (((1,), (1,)), ((), ())), preferred_element_type=jnp.float32)


def dot_tn(a, b):
    return lax.dot_general(a, b, (((0,), (0,)), ((), ())), preferred_element_type=jnp.float32)


def one_side(query, key_rows, val_rows, grad_out, mask):
    factor = HD ** (-0.5)
    scores = jnp.where(mask, dot_nt(query, key_rows) * factor, NEG_BIG)
    exponent = jnp.exp(scores - jnp.max(scores, axis=-1, keepdims=True))
    weights = exponent / jnp.sum(exponent, axis=-1, keepdims=True)
    half = weights.astype(jnp.bfloat16)
    output = jnp.dot(half, val_rows, preferred_element_type=jnp.float32)
    deltas = jnp.sum(grad_out.astype(jnp.float32) * output, axis=-1, keepdims=True)
    grad_weights = dot_nt(grad_out, val_rows)
    grad_scores = (weights * (grad_weights - deltas)).astype(jnp.bfloat16)
    grad_query = jnp.dot(grad_scores, key_rows, preferred_element_type=jnp.float32) * factor
    key_terms = dot_tn(grad_scores, query) * factor
    val_terms = dot_tn(half, grad_out)
    return tuple(x.astype(jnp.bfloat16) for x in (grad_query, key_terms, val_terms))


def block_kernel(heads, vr, ar, seq_count, match_ref, len_ref, here_ref, vq_ref, aq_ref, *refs):
    videos, audios = refs[:SPAN], refs[SPAN : 2 * SPAN]
    gvq_ref, gaq_ref = refs[2 * SPAN : 2 * SPAN + 2]
    video_terms = refs[2 * SPAN + 2 : 3 * SPAN + 2]
    audio_terms = refs[3 * SPAN + 2 :]
    group = match_ref[pl.program_id(0)]
    here = here_ref[0]
    slot = lax.broadcasted_iota(jnp.int32, (vr, SPAN * ar), 1)
    token = lax.broadcasted_iota(jnp.int32, (ar, SPAN * vr), 1)
    audio_live = slot < 0
    video_live = token < 0
    for p in range(SPAN):
        at = here + (p - BAND)
        inside = (at >= 0) & (at < seq_count)
        length = jnp.where(inside, len_ref[group, jnp.clip(at, 0, seq_count - 1)], 0)
        audio_live |= (slot >= p * ar) & (slot < p * ar + length)
        video_live |= (token >= p * vr) & (token < p * vr + jnp.where(inside, vr, 0))
    row = lax.broadcasted_iota(jnp.int32, (ar, HD), 0)
    own_live = row < len_ref[group, here]
    for h in range(heads):
        cols = slice(h * HD, (h + 1) * HD)
        grad, keys, vals = one_side(
            vq_ref[0, :vr, cols],
            jnp.concatenate([r[0, :ar, cols] for r in audios], axis=0),
            jnp.concatenate([r[0, ar:, cols] for r in audios], axis=0),
            vq_ref[0, vr:, cols],
            audio_live,
        )
        gvq_ref[0, :, cols] = grad
        for p in range(SPAN):
            audio_terms[p][0, :ar, cols] = keys[p * ar : (p + 1) * ar]
            audio_terms[p][0, ar:, cols] = vals[p * ar : (p + 1) * ar]
        audio_grad = aq_ref[0, ar:, cols]
        grad, keys, vals = one_side(
            aq_ref[0, :ar, cols],
            jnp.concatenate([r[0, :vr, cols] for r in videos], axis=0),
            jnp.concatenate([r[0, vr:, cols] for r in videos], axis=0),
            jnp.where(own_live, audio_grad, jnp.zeros_like(audio_grad)),
            video_live,
        )
        gaq_ref[0, :, cols] = grad
        for p in range(SPAN):
            video_terms[p][0, :vr, cols] = keys[p * vr : (p + 1) * vr]
            video_terms[p][0, vr:, cols] = vals[p * vr : (p + 1) * vr]


def spread(arrays, frames):
    rows = jnp.concatenate([a[0] for a in arrays], axis=0)
    width = rows.shape[1] // frames
    cut = jnp.stack([rows[:, i * width : (i + 1) * width] for i in range(frames)])
    return lax.all_to_all(cut, "frame", split_axis=0, concat_axis=0, tiled=True)


def shards(vid_q, vid_k, vid_v, vid_dout, aud_q, aud_k, aud_v, aud_dout, aud_len, match):
    frames = lax.axis_size("frame")
    seq_count = lax.axis_size("seq")
    here = lax.axis_index("seq").astype(jnp.int32).reshape(1)
    vr, ar = vid_q.shape[1], aud_q.shape[1]
    width = vid_q.shape[2] // frames
    offsets = range(-BAND, BAND + 1)
    sources = spread((aud_k, aud_v, vid_k, vid_v), frames)
    queries = spread((aud_q, aud_dout, vid_q, vid_dout), frames)
    nearby = [sources if o == 0 else from_behind(sources, "seq", -o) for o in offsets]

    tail = 2 * ar // (2 * vr)
    video_rows = pl.BlockSpec((1, 2 * vr, width), lambda f, m, l, w: (f, tail, 0))
    audio_rows = pl.BlockSpec((1, 2 * ar, width), lambda f, m, l, w: (m[f], 0, 0))
    video_own = pl.BlockSpec((1, 2 * vr, width), lambda f, m, l, w: (f, 0, 0))
    gvq_spec = pl.BlockSpec((1, vr, width), lambda f, m, l, w: (f, 0, 0))
    gaq_spec = pl.BlockSpec((1, ar, width), lambda f, m, l, w: (m[f], 0, 0))

    def like(rows):
        return jax.ShapeDtypeStruct((frames, rows, width), jnp.bfloat16)

    flops = 2 * 6 * frames * width * 2 * vr * SPAN * ar
    outs = pl.pallas_call(
        functools.partial(block_kernel, width // HD, vr, ar, seq_count),
        out_shape=[like(vr), like(ar)] + [like(2 * vr)] * SPAN + [like(2 * ar)] * SPAN,
        grid_spec=pltpu.PrefetchScalarGridSpec(
            num_scalar_prefetch=3,
            grid=(frames,),
            in_specs=[video_rows, audio_rows] + [video_rows] * SPAN + [audio_rows] * SPAN,
            out_specs=[gvq_spec, gaq_spec] + [video_own] * SPAN + [audio_rows] * SPAN,
        ),
        compiler_params=pltpu.CompilerParams(vmem_limit_bytes=48 * 2**20),
        cost_estimate=pl.CostEstimate(
            flops=flops, bytes_accessed=12 * 2**20, transcendentals=flops // (12 * HD)
        ),
    )(match, aud_len, here, queries, queries, *nearby, *nearby)
    grad_vq, grad_aq = outs[:2]
    video_terms, audio_terms = outs[2 : 2 + SPAN], outs[2 + SPAN :]

    def gathered(terms):
        total = terms[BAND].astype(jnp.float32)
        for position, offset in enumerate(offsets):
            if offset != 0:
                total = total + from_behind(terms[position], "seq", offset).astype(jnp.float32)
        return total.astype(jnp.bfloat16)

    packed = jnp.concatenate(
        [gathered(audio_terms), grad_aq, gathered(video_terms), grad_vq], axis=1
    )
    back = lax.all_to_all(packed, "frame", split_axis=0, concat_axis=0, tiled=True)

    def whole(start, rows):
        parts = [back[i, start : start + rows] for i in range(frames)]
        return jnp.concatenate(parts, axis=1)[None]

    base = 3 * ar
    return (
        whole(base + 2 * vr, vr),
        whole(base, vr),
        whole(base + vr, vr),
        whole(2 * ar, ar),
        whole(0, ar),
        whole(ar, ar),
    )


def solution(mesh):
    token = P("frame", "seq", None)
    return jax.shard_map(
        shards,
        mesh=mesh,
        in_specs=(token,) * 8 + (P(), P()),
        out_specs=(token,) * 6,
        check_vma=False,
    )
```

```python
import functools

import jax
import jax.numpy as jnp
from jax import lax
from jax.experimental import pallas as pl
from jax.experimental.pallas import tpu as pltpu
from jax.sharding import PartitionSpec as P

HD = 128
BAND = 2
SPAN = 2 * BAND + 1
NEG_BIG = -1e30


def from_behind(x, axis, by):
    peers = lax.axis_size(axis)
    pairs = [(i, i + by) for i in range(peers) if 0 <= i + by < peers]
    return lax.ppermute(x, axis, pairs)


def dot_nt(a, b):
    return lax.dot_general(a, b, (((1,), (1,)), ((), ())), preferred_element_type=jnp.float32)


def dot_tn(a, b):
    return lax.dot_general(a, b, (((0,), (0,)), ((), ())), preferred_element_type=jnp.float32)


def one_side(query, key_rows, val_rows, grad_out, mask):
    factor = HD ** (-0.5)
    scores = jnp.where(mask, dot_nt(query, key_rows) * factor, NEG_BIG)
    exponent = jnp.exp(scores - jnp.max(scores, axis=-1, keepdims=True))
    weights = exponent / jnp.sum(exponent, axis=-1, keepdims=True)
    half = weights.astype(jnp.bfloat16)
    output = jnp.dot(half, val_rows, preferred_element_type=jnp.float32)
    deltas = jnp.sum(grad_out.astype(jnp.float32) * output, axis=-1, keepdims=True)
    grad_weights = dot_nt(grad_out, val_rows)
    grad_scores = (weights * (grad_weights - deltas)).astype(jnp.bfloat16)
    grad_query = jnp.dot(grad_scores, key_rows, preferred_element_type=jnp.float32) * factor
    key_terms = dot_tn(grad_scores, query) * factor
    val_terms = dot_tn(half, grad_out)
    return tuple(x.astype(jnp.bfloat16) for x in (grad_query, key_terms, val_terms))


def block_kernel(frames, heads, vr, ar, seq_count, match_ref, len_ref, here_ref, own_ref, *refs):
    near, back_ref, terms = refs[:SPAN], refs[SPAN], refs[SPAN + 1 :]
    here = here_ref[0]
    split = 2 * ar
    slot = lax.broadcasted_iota(jnp.int32, (vr, SPAN * ar), 1)
    token = lax.broadcasted_iota(jnp.int32, (ar, SPAN * vr), 1)
    row = lax.broadcasted_iota(jnp.int32, (ar, HD), 0)

    def pair(f, carry):
        group = match_ref[f]
        audio_live = slot < 0
        video_live = token < 0
        for p in range(SPAN):
            at = here + (p - BAND)
            inside = (at >= 0) & (at < seq_count)
            length = jnp.where(inside, len_ref[group, jnp.clip(at, 0, seq_count - 1)], 0)
            audio_live |= (slot >= p * ar) & (slot < p * ar + length)
            video_live |= (token >= p * vr) & (token < p * vr + jnp.where(inside, vr, 0))
        own_live = row < len_ref[group, here]
        for h in range(heads):
            cols = slice(h * HD, (h + 1) * HD)
            grad, keys, vals = one_side(
                own_ref[f, split : split + vr, cols],
                jnp.concatenate([r[group, :ar, cols] for r in near], axis=0),
                jnp.concatenate([r[group, ar:split, cols] for r in near], axis=0),
                own_ref[f, split + vr :, cols],
                audio_live,
            )
            back_ref[f, ar:, cols] = grad
            for p in range(SPAN):
                terms[p][group, :ar, cols] = keys[p * ar : (p + 1) * ar]
                terms[p][group, ar:split, cols] = vals[p * ar : (p + 1) * ar]
            audio_grad = own_ref[group, ar:split, cols]
            grad, keys, vals = one_side(
                own_ref[group, :ar, cols],
                jnp.concatenate([r[f, split : split + vr, cols] for r in near], axis=0),
                jnp.concatenate([r[f, split + vr :, cols] for r in near], axis=0),
                jnp.where(own_live, audio_grad, jnp.zeros_like(audio_grad)),
                video_live,
            )
            back_ref[group, :ar, cols] = grad
            for p in range(SPAN):
                terms[p][f, split : split + vr, cols] = keys[p * vr : (p + 1) * vr]
                terms[p][f, split + vr :, cols] = vals[p * vr : (p + 1) * vr]
        return carry

    lax.fori_loop(0, frames, pair, 0)


def spread(arrays, frames):
    rows = jnp.concatenate([a[0] for a in arrays], axis=0)
    width = rows.shape[1] // frames
    cut = jnp.stack([rows[:, i * width : (i + 1) * width] for i in range(frames)])
    return lax.all_to_all(cut, "frame", split_axis=0, concat_axis=0, tiled=True)


def shards(vid_q, vid_k, vid_v, vid_dout, aud_q, aud_k, aud_v, aud_dout, aud_len, match):
    frames = lax.axis_size("frame")
    seq_count = lax.axis_size("seq")
    here = lax.axis_index("seq").astype(jnp.int32).reshape(1)
    vr, ar = vid_q.shape[1], aud_q.shape[1]
    width = vid_q.shape[2] // frames
    offsets = range(-BAND, BAND + 1)
    sources = spread((aud_k, aud_v, vid_k, vid_v), frames)
    queries = spread((aud_q, aud_dout, vid_q, vid_dout), frames)
    nearby = [sources if o == 0 else from_behind(sources, "seq", -o) for o in offsets]

    def like(rows):
        return jax.ShapeDtypeStruct((frames, rows, width), jnp.bfloat16)

    flops = 2 * 6 * frames * width * 2 * vr * SPAN * ar
    scalars = [pl.BlockSpec(memory_space=pltpu.SMEM)] * 3
    outs = pl.pallas_call(
        functools.partial(block_kernel, frames, width // HD, vr, ar, seq_count),
        out_shape=[like(vr + ar)] + [like(2 * (vr + ar))] * SPAN,
        in_specs=scalars + [pl.BlockSpec(memory_space=pltpu.VMEM)] * (1 + SPAN),
        out_specs=[pl.BlockSpec(memory_space=pltpu.VMEM)] * (1 + SPAN),
        compiler_params=pltpu.CompilerParams(vmem_limit_bytes=48 * 2**20),
        cost_estimate=pl.CostEstimate(
            flops=flops, bytes_accessed=12 * 2**20, transcendentals=flops // (12 * HD)
        ),
    )(match, aud_len, here, queries, *nearby)
    grads, terms = outs[0], outs[1:]

    def gathered(terms):
        total = terms[BAND].astype(jnp.float32)
        for position, offset in enumerate(offsets):
            if offset != 0:
                total = total + from_behind(terms[position], "seq", offset).astype(jnp.float32)
        return total.astype(jnp.bfloat16)

    packed = jnp.concatenate([gathered(terms), grads], axis=1)
    back = lax.all_to_all(packed, "frame", split_axis=0, concat_axis=0, tiled=True)

    def whole(start, rows):
        parts = [back[i, start : start + rows] for i in range(frames)]
        return jnp.concatenate(parts, axis=1)[None]

    base = 2 * (ar + vr)
    return (
        whole(base + ar, vr),
        whole(2 * ar, vr),
        whole(2 * ar + vr, vr),
        whole(base, ar),
        whole(0, ar),
        whole(ar, ar),
    )


def solution(mesh):
    token = P("frame", "seq", None)
    return jax.shard_map(
        shards,
        mesh=mesh,
        in_specs=(token,) * 8 + (P(), P()),
        out_specs=(token,) * 6,
        check_vma=False,
    )
```

```python
import functools

import jax
import jax.numpy as jnp
from jax import lax
from jax.experimental import pallas as pl
from jax.experimental.pallas import tpu as pltpu
from jax.sharding import PartitionSpec as P

HD = 128
BAND = 2
SPAN = 2 * BAND + 1
NEG_BIG = -1e30


def from_behind(x, axis, by):
    peers = lax.axis_size(axis)
    pairs = [(i, i + by) for i in range(peers) if 0 <= i + by < peers]
    return lax.ppermute(x, axis, pairs)


def to_partner(x, axis):
    peers = lax.axis_size(axis)
    return lax.ppermute(x, axis, [(i, i ^ 1) for i in range(peers)])


def dot_nt(a, b):
    return lax.dot_general(a, b, (((1,), (1,)), ((), ())), preferred_element_type=jnp.float32)


def dot_tn(a, b):
    return lax.dot_general(a, b, (((0,), (0,)), ((), ())), preferred_element_type=jnp.float32)


def one_side(query, key_rows, val_rows, grad_out, mask):
    factor = HD ** (-0.5)
    scores = jnp.where(mask, dot_nt(query, key_rows) * factor, NEG_BIG)
    exponent = jnp.exp(scores - jnp.max(scores, axis=-1, keepdims=True))
    weights = exponent / jnp.sum(exponent, axis=-1, keepdims=True)
    half = weights.astype(jnp.bfloat16)
    output = jnp.dot(half, val_rows, preferred_element_type=jnp.float32)
    deltas = jnp.sum(grad_out.astype(jnp.float32) * output, axis=-1, keepdims=True)
    grad_weights = dot_nt(grad_out, val_rows)
    grad_scores = (weights * (grad_weights - deltas)).astype(jnp.bfloat16)
    grad_query = jnp.dot(grad_scores, key_rows, preferred_element_type=jnp.float32) * factor
    key_terms = dot_tn(grad_scores, query) * factor
    val_terms = dot_tn(half, grad_out)
    return tuple(x.astype(jnp.bfloat16) for x in (grad_query, key_terms, val_terms))


def block_kernel(frames, heads, vr, ar, seq_count, match_ref, len_ref, here_ref, own_ref, *refs):
    near, back_ref = refs[:SPAN], refs[SPAN]
    far_behind, sides, centre, far_ahead = refs[SPAN + 1 :]
    terms = (far_behind, sides.at[0], centre, sides.at[1], far_ahead)
    here = here_ref[0]
    split = 2 * ar
    slot = lax.broadcasted_iota(jnp.int32, (vr, SPAN * ar), 1)
    token = lax.broadcasted_iota(jnp.int32, (ar, SPAN * vr), 1)
    row = lax.broadcasted_iota(jnp.int32, (ar, HD), 0)

    def pair(f, carry):
        group = match_ref[f]
        audio_live = slot < 0
        video_live = token < 0
        for p in range(SPAN):
            at = here + (p - BAND)
            inside = (at >= 0) & (at < seq_count)
            length = jnp.where(inside, len_ref[group, jnp.clip(at, 0, seq_count - 1)], 0)
            audio_live |= (slot >= p * ar) & (slot < p * ar + length)
            video_live |= (token >= p * vr) & (token < p * vr + jnp.where(inside, vr, 0))
        own_live = row < len_ref[group, here]
        for h in range(heads):
            cols = slice(h * HD, (h + 1) * HD)
            grad, keys, vals = one_side(
                own_ref[f, split : split + vr, cols],
                jnp.concatenate([r[group, :ar, cols] for r in near], axis=0),
                jnp.concatenate([r[group, ar:split, cols] for r in near], axis=0),
                own_ref[f, split + vr :, cols],
                audio_live,
            )
            back_ref[f, ar:, cols] = grad
            for p in range(SPAN):
                terms[p][group, :ar, cols] = keys[p * ar : (p + 1) * ar]
                terms[p][group, ar:split, cols] = vals[p * ar : (p + 1) * ar]
            audio_grad = own_ref[group, ar:split, cols]
            grad, keys, vals = one_side(
                own_ref[group, :ar, cols],
                jnp.concatenate([r[f, split : split + vr, cols] for r in near], axis=0),
                jnp.concatenate([r[f, split + vr :, cols] for r in near], axis=0),
                jnp.where(own_live, audio_grad, jnp.zeros_like(audio_grad)),
                video_live,
            )
            back_ref[group, :ar, cols] = grad
            for p in range(SPAN):
                terms[p][f, split : split + vr, cols] = keys[p * vr : (p + 1) * vr]
                terms[p][f, split + vr :, cols] = vals[p * vr : (p + 1) * vr]
        return carry

    lax.fori_loop(0, frames, pair, 0)


def spread(arrays, frames):
    rows = jnp.concatenate([a[0] for a in arrays], axis=0)
    width = rows.shape[1] // frames
    cut = jnp.stack([rows[:, i * width : (i + 1) * width] for i in range(frames)])
    return lax.all_to_all(cut, "frame", split_axis=0, concat_axis=0, tiled=True)


def shards(vid_q, vid_k, vid_v, vid_dout, aud_q, aud_k, aud_v, aud_dout, aud_len, match):
    frames = lax.axis_size("frame")
    seq_count = lax.axis_size("seq")
    here = lax.axis_index("seq").astype(jnp.int32).reshape(1)
    vr, ar = vid_q.shape[1], aud_q.shape[1]
    width = vid_q.shape[2] // frames
    sources = spread((aud_k, aud_v, vid_k, vid_v), frames)
    queries = spread((aud_q, aud_dout, vid_q, vid_dout), frames)
    even = lax.rem(lax.axis_index("seq"), 2) == 0
    offsets = range(-BAND, BAND + 1)
    nearby = [sources if o == 0 else from_behind(sources, "seq", -o) for o in offsets]

    def like(rows):
        return jax.ShapeDtypeStruct((frames, rows, width), jnp.bfloat16)

    term = like(2 * (vr + ar))
    both = jax.ShapeDtypeStruct((2,) + term.shape, term.dtype)
    flops = 2 * 6 * frames * width * 2 * vr * SPAN * ar
    scalars = [pl.BlockSpec(memory_space=pltpu.SMEM)] * 3
    outs = pl.pallas_call(
        functools.partial(block_kernel, frames, width // HD, vr, ar, seq_count),
        out_shape=[like(vr + ar), term, both, term, term],
        in_specs=scalars + [pl.BlockSpec(memory_space=pltpu.VMEM)] * (1 + SPAN),
        out_specs=[pl.BlockSpec(memory_space=pltpu.VMEM)] * 5,
        compiler_params=pltpu.CompilerParams(vmem_limit_bytes=48 * 2**20),
        cost_estimate=pl.CostEstimate(
            flops=flops, bytes_accessed=12 * 2**20, transcendentals=flops // (12 * HD)
        ),
    )(match, aud_len, here, queries, *nearby)
    grads, far_behind, sides, centre, far_ahead = outs
    got = to_partner(sides, "seq")

    def wide(x):
        return x.astype(jnp.float32)

    sent_ahead = wide(far_ahead) + jnp.where(even, wide(got[1]), 0.0)
    sent_behind = wide(far_behind) + jnp.where(even, 0.0, wide(got[0]))
    total = wide(centre) + wide(jnp.where(even, got[0], got[1]))
    total = total + wide(from_behind(sent_ahead.astype(jnp.bfloat16), "seq", BAND))
    total = total + wide(from_behind(sent_behind.astype(jnp.bfloat16), "seq", -BAND))
    packed = jnp.concatenate([total.astype(jnp.bfloat16), grads], axis=1)
    back = lax.all_to_all(packed, "frame", split_axis=0, concat_axis=0, tiled=True)

    def whole(start, rows):
        parts = [back[i, start : start + rows] for i in range(frames)]
        return jnp.concatenate(parts, axis=1)[None]

    base = 2 * (ar + vr)
    return (
        whole(base + ar, vr),
        whole(2 * ar, vr),
        whole(2 * ar + vr, vr),
        whole(base, ar),
        whole(0, ar),
        whole(ar, ar),
    )


def solution(mesh):
    token = P("frame", "seq", None)
    return jax.shard_map(
        shards,
        mesh=mesh,
        in_specs=(token,) * 8 + (P(), P()),
        out_specs=(token,) * 6,
        check_vma=False,
    )
```

```python
import functools

import jax
import jax.numpy as jnp
from jax import lax
from jax.experimental import pallas as pl
from jax.experimental.pallas import tpu as pltpu
from jax.sharding import PartitionSpec as P

HD = 128
BAND = 2
SPAN = 2 * BAND + 1
NEG_BIG = -1e30


def from_behind(x, axis, by):
    peers = lax.axis_size(axis)
    pairs = [(i, i + by) for i in range(peers) if 0 <= i + by < peers]
    return lax.ppermute(x, axis, pairs)


def to_partner(x, axis):
    peers = lax.axis_size(axis)
    return lax.ppermute(x, axis, [(i, i ^ 1) for i in range(peers)])


def dot_nt(a, b):
    return lax.dot_general(a, b, (((1,), (1,)), ((), ())), preferred_element_type=jnp.float32)


def dot_tn(a, b):
    return lax.dot_general(a, b, (((0,), (0,)), ((), ())), preferred_element_type=jnp.float32)


def one_side(query, key_rows, val_rows, grad_out, mask):
    factor = HD ** (-0.5)
    scores = jnp.where(mask, dot_nt(query, key_rows) * factor, NEG_BIG)
    exponent = jnp.exp(scores - jnp.max(scores, axis=-1, keepdims=True))
    weights = exponent / jnp.sum(exponent, axis=-1, keepdims=True)
    half = weights.astype(jnp.bfloat16)
    output = jnp.dot(half, val_rows, preferred_element_type=jnp.float32)
    deltas = jnp.sum(grad_out.astype(jnp.float32) * output, axis=-1, keepdims=True)
    grad_weights = dot_nt(grad_out, val_rows)
    grad_scores = (weights * (grad_weights - deltas)).astype(jnp.bfloat16)
    grad_query = jnp.dot(grad_scores, key_rows, preferred_element_type=jnp.float32) * factor
    key_terms = dot_tn(grad_scores, query) * factor
    val_terms = dot_tn(half, grad_out)
    return tuple(x.astype(jnp.bfloat16) for x in (grad_query, key_terms, val_terms))


def block_kernel(frames, heads, vr, ar, seq_count, match_ref, len_ref, here_ref, own_ref, *refs):
    near, back_ref, terms = refs[:SPAN][::-1], refs[SPAN], refs[SPAN + 1 :]
    here = here_ref[0]
    split = 2 * ar
    slot = lax.broadcasted_iota(jnp.int32, (vr, SPAN * ar), 1)
    token = lax.broadcasted_iota(jnp.int32, (ar, SPAN * vr), 1)
    row = lax.broadcasted_iota(jnp.int32, (ar, HD), 0)

    def pair(f, carry):
        group = match_ref[f]
        audio_live = slot < 0
        video_live = token < 0
        for p in range(SPAN):
            at = here + (p - BAND)
            inside = (at >= 0) & (at < seq_count)
            length = jnp.where(inside, len_ref[group, jnp.clip(at, 0, seq_count - 1)], 0)
            audio_live |= (slot >= p * ar) & (slot < p * ar + length)
            video_live |= (token >= p * vr) & (token < p * vr + jnp.where(inside, vr, 0))
        own_live = row < len_ref[group, here]
        for h in range(heads):
            cols = slice(h * HD, (h + 1) * HD)
            grad, keys, vals = one_side(
                own_ref[f, split : split + vr, cols],
                jnp.concatenate([r[group, :ar, cols] for r in near], axis=0),
                jnp.concatenate([r[group, ar:split, cols] for r in near], axis=0),
                own_ref[f, split + vr :, cols],
                audio_live,
            )
            back_ref[f, ar:, cols] = grad
            for p in range(SPAN):
                terms[p][group, :ar, cols] = keys[p * ar : (p + 1) * ar]
                terms[p][group, ar:split, cols] = vals[p * ar : (p + 1) * ar]
            audio_grad = own_ref[group, ar:split, cols]
            grad, keys, vals = one_side(
                own_ref[group, :ar, cols],
                jnp.concatenate([r[f, split : split + vr, cols] for r in near], axis=0),
                jnp.concatenate([r[f, split + vr :, cols] for r in near], axis=0),
                jnp.where(own_live, audio_grad, jnp.zeros_like(audio_grad)),
                video_live,
            )
            back_ref[group, :ar, cols] = grad
            for p in range(SPAN):
                terms[p][f, split : split + vr, cols] = keys[p * vr : (p + 1) * vr]
                terms[p][f, split + vr :, cols] = vals[p * vr : (p + 1) * vr]
        return carry

    lax.fori_loop(0, frames, pair, 0)


def spread(arrays, frames):
    rows = jnp.concatenate([a[0] for a in arrays], axis=0)
    width = rows.shape[1] // frames
    cut = jnp.stack([rows[:, i * width : (i + 1) * width] for i in range(frames)])
    return lax.all_to_all(cut, "frame", split_axis=0, concat_axis=0, tiled=True)


def shards(vid_q, vid_k, vid_v, vid_dout, aud_q, aud_k, aud_v, aud_dout, aud_len, match):
    frames = lax.axis_size("frame")
    seq_count = lax.axis_size("seq")
    here = lax.axis_index("seq").astype(jnp.int32).reshape(1)
    vr, ar = vid_q.shape[1], aud_q.shape[1]
    width = vid_q.shape[2] // frames
    sources = spread((aud_k, aud_v, vid_k, vid_v), frames)
    queries = spread((aud_q, aud_dout, vid_q, vid_dout), frames)
    even = lax.rem(lax.axis_index("seq"), 2) == 0
    offsets = range(-BAND, BAND + 1)
    nearby = [sources if o == 0 else from_behind(sources, "seq", -o) for o in reversed(offsets)]

    def like(rows):
        return jax.ShapeDtypeStruct((frames, rows, width), jnp.bfloat16)

    flops = 2 * 6 * frames * width * 2 * vr * SPAN * ar
    scalars = [pl.BlockSpec(memory_space=pltpu.SMEM)] * 3
    outs = pl.pallas_call(
        functools.partial(block_kernel, frames, width // HD, vr, ar, seq_count),
        out_shape=[like(vr + ar)] + [like(2 * (vr + ar))] * SPAN,
        in_specs=scalars + [pl.BlockSpec(memory_space=pltpu.VMEM)] * (1 + SPAN),
        out_specs=[pl.BlockSpec(memory_space=pltpu.VMEM)] * (1 + SPAN),
        compiler_params=pltpu.CompilerParams(vmem_limit_bytes=48 * 2**20),
        cost_estimate=pl.CostEstimate(
            flops=flops, bytes_accessed=12 * 2**20, transcendentals=flops // (12 * HD)
        ),
    )(match, aud_len, here, queries, *nearby)
    grads, far_behind, near_behind, centre, near_ahead, far_ahead = outs
    got = (to_partner(near_behind, "seq"), to_partner(near_ahead, "seq"))

    def wide(x):
        return x.astype(jnp.float32)

    sent_ahead = wide(far_ahead) + jnp.where(even, wide(got[1]), 0.0)
    sent_behind = wide(far_behind) + jnp.where(even, 0.0, wide(got[0]))
    total = wide(centre) + wide(jnp.where(even, got[0], got[1]))
    total = total + wide(from_behind(sent_ahead.astype(jnp.bfloat16), "seq", BAND))
    total = total + wide(from_behind(sent_behind.astype(jnp.bfloat16), "seq", -BAND))
    packed = jnp.concatenate([total.astype(jnp.bfloat16), grads], axis=1)
    back = lax.all_to_all(packed, "frame", split_axis=0, concat_axis=0, tiled=True)

    def whole(start, rows):
        parts = [back[i, start : start + rows] for i in range(frames)]
        return jnp.concatenate(parts, axis=1)[None]

    base = 2 * (ar + vr)
    return (
        whole(base + ar, vr),
        whole(2 * ar, vr),
        whole(2 * ar + vr, vr),
        whole(base, ar),
        whole(0, ar),
        whole(ar, ar),
    )


def solution(mesh):
    token = P("frame", "seq", None)
    return jax.shard_map(
        shards,
        mesh=mesh,
        in_specs=(token,) * 8 + (P(), P()),
        out_specs=(token,) * 6,
        check_vma=False,
    )
```
